32 devices in a mesh: row: 4 (over x, core), col: 8 (over z, y).
Axes of the slice: x: 2, y: 2, z: 4, core: 2. Of those that a mesh axis runs over, the one named last changes fastest.
Arguments:
- amplitudes: bfloat16 [8, 8, 768, 768], P('row', 'col'), may hold values from -0.59765625 to 0.59765625
- ints: bfloat16 [8, 768, 2304], P('row', None, 'col'), may hold values from -0.3984375 to 0.3984375
- eps_occ: float32 [8], replicated, may hold values from -2 to -0.5
- eps_vir: float32 [768], replicated, may hold values from 0.2 to 3
- fock_vir: bfloat16 [768, 768], replicated, may hold values from -2 to 2, as said below
Outputs:
- updated: bfloat16 [8, 8, 768, 768], P('row', 'col')
The draws below stay inside these ranges and needn't reach their ends.
Inputs may be any that keep to these rules, and one draw needn't show every extreme that they name: fock_vir is zero on its diagonal.
All inputs are finite; a program needn't handle non-finite values.
Results may differ from the reference program's by a relative error of at most 0.019.
Values may be sent and summed in bfloat16 or wider, within the bound.
No kernel may reach another device: no remote copies, remote signals or barrier semaphores. Data moves between devices by JAX's collectives and lax.ppermute only.
A program may use at most 64 MiB of HBM per device.

```python
import jax
import jax.numpy as jnp
from jax import lax

V = 768
NAUX = 2304
O = 8


def draw_fock_vir(key, part):
    own_key = jax.random.fold_in(key, 7301)
    spread = 1.0 / jnp.sqrt(jnp.float32(V // 16))
    limit = jnp.minimum(jnp.float32(2.0), 6.0 * spread)
    values = jax.random.normal(own_key, (V, V), jnp.float32) * spread
    values = jnp.clip(values, -limit, limit)
    off_diag = 1.0 - jnp.eye(V, dtype=jnp.float32)
    return (values * off_diag).astype(jnp.bfloat16)


def block_levels(stream_key, shape, pieces, low, top_value):
    gain, own = 1.0, jax.random.fold_in(stream_key, 6)
    for position, blocks in pieces:
        heights = jnp.exp(jax.random.uniform(jax.random.fold_in(own, position), (blocks,), jnp.float32, low / len(pieces), top_value / len(pieces)))
        gain = gain * jnp.repeat(heights, shape[position] // blocks).reshape([-1 if axis == position else 1 for axis in range(len(shape))])
    return gain


def normal_values(key, extent, deviation, bound, shards=(), kind=jnp.bfloat16):
    factor_of = block_levels(key, extent, shards, -0.22, 0.18) if shards else 1.0
    array = jax.random.normal(key, extent, jnp.float32) * deviation * factor_of
    return jnp.minimum(jnp.maximum(array, -bound), bound).astype(kind)


def setup_inputs(seed: int = 0) -> dict:
    arg_keys = jax.random.split(jax.random.key(seed), 6)
    return {
        "amplitudes": normal_values(arg_keys[0], (O, O, V, V), 0.1, 0.59765625, ((0, 4), (1, 8))),
        "ints": normal_values(arg_keys[1], (O, V, NAUX), 0.066, 0.3984375, ((0, 4), (2, 8))),
        "eps_occ": jnp.clip(jax.random.uniform(arg_keys[2], (O,), jnp.float32, -2.0, -0.5), -2.0, -0.5),
        "eps_vir": jnp.clip(jax.random.uniform(arg_keys[3], (V,), jnp.float32, 0.2, 3.0), 0.2, 3.0),
        "fock_vir": draw_fock_vir(jax.random.fold_in(arg_keys[5], 71), 0),
    }


def reference(amplitudes, ints, eps_occ, eps_vir, fock_vir):
    occ = ints.shape[0]
    vir = ints.shape[1]
    aux = ints.shape[2]
    flat_ints = ints.reshape(occ * vir, aux)

    def one_column(column):
        amp_col = lax.dynamic_index_in_dim(amplitudes, column, 1, keepdims=False)
        flat_amp = amp_col.reshape(occ * vir, vir)
        cross = jnp.dot(flat_amp.T, flat_ints, preferred_element_type=jnp.float32)
        own = lax.dynamic_index_in_dim(ints, column, 0, keepdims=False)
        dressed = (own.astype(jnp.float32) + cross).astype(jnp.bfloat16)
        pair = jnp.dot(flat_ints, dressed.T, preferred_element_type=jnp.float32).reshape(occ, vir, vir)
        fock_term = jnp.dot(flat_amp, fock_vir, preferred_element_type=jnp.float32).reshape(occ, vir, vir)
        numer = pair + fock_term
        eps_col = lax.dynamic_index_in_dim(eps_occ, column, 0, keepdims=False)
        denom = eps_vir[None, :, None] + eps_vir[None, None, :] - eps_occ[:, None, None] - eps_col
        return (amp_col.astype(jnp.float32) - numer / denom).astype(jnp.bfloat16)

    columns = lax.map(one_column, jnp.arange(occ, dtype=jnp.int32))
    return jnp.transpose(columns, (1, 0, 2, 3))
```

```python
import functools

import jax
import jax.numpy as jnp
from jax import lax
from jax.experimental import pallas as pl
from jax.experimental.pallas import tpu as pltpu
from jax.sharding import PartitionSpec as P

VMEM_LIMIT = 56 * 1024 * 1024


def ring_order(n):
    low = max(d for d in range(1, n + 1) if n % d == 0 and d * d <= n)
    high = n // low
    if low == 1 or high % 2:
        return list(range(n))
    order = [h * low for h in range(high)]
    for turn, h in enumerate(reversed(range(high))):
        lows = range(1, low) if turn % 2 == 0 else range(low - 1, 0, -1)
        order += [h * low + l for l in lows]
    return order


def group_sizes(total):
    sizes = []
    size = 1
    while total:
        sizes.append(min(size, total))
        total -= sizes[-1]
        if len(sizes) > 1:
            size *= 2
    return sizes[::-1]


def cross_kernel(flags, t_ref, *refs):
    chunks, (keep_ref, send_ref, full) = refs[:-3], refs[-3:]
    occ, vir = t_ref.shape[0], t_ref.shape[2]
    half = vir // 2
    for start in range(0, vir, 256):
        cols = slice(start, min(start + 256, vir))
        total = None
        for k in range(occ):
            rows = jnp.concatenate([c[k] for c in chunks], axis=0)
            part = jnp.dot(rows, t_ref[k, :, cols], preferred_element_type=jnp.float32)
            own = jnp.concatenate([c[k, :, cols] for c in chunks], axis=0).astype(jnp.float32)
            part = part + jnp.where(flags[1 + k] == 1, own, 0.0)
            total = part if total is None else total + part
        full[:, cols] = total
    low, high = full[:, :half], full[:, half:]
    first = flags[0] == 0
    keep_ref[...] = jnp.where(first, low, high)
    send_ref[...] = jnp.where(first, high, low).astype(send_ref.dtype)


def cross(flags, t, chunks):
    rows = sum(c.shape[1] for c in chunks)
    vir = t.shape[2]
    vmem = pl.BlockSpec(memory_space=pltpu.VMEM)
    return pl.pallas_call(
        cross_kernel,
        out_shape=(
            jax.ShapeDtypeStruct((rows, vir // 2), jnp.float32),
            jax.ShapeDtypeStruct((rows, vir // 2), jnp.bfloat16),
        ),
        in_specs=[pl.BlockSpec(memory_space=pltpu.SMEM)] + [vmem] * (1 + len(chunks)),
        out_specs=(vmem, vmem),
        scratch_shapes=[pltpu.VMEM((rows, vir), jnp.float32)],
        compiler_params=pltpu.CompilerParams(vmem_limit_bytes=VMEM_LIMIT),
        cost_estimate=pl.CostEstimate(
            flops=2 * rows * vir * vir * t.shape[0],
            bytes_accessed=2 * t.size + 2 * rows * vir * (t.shape[0] + 2),
            transcendentals=0,
        ),
        name="cross",
    )(flags, t, *chunks)


def joined(first, mine, other):
    return jnp.concatenate(
        [jnp.where(first, mine, other), jnp.where(first, other, mine)], axis=1
    )


def numer_kernel(counts, flags, t_ref, fock_ref, *refs):
    groups = len(counts)
    chunks = refs[: sum(counts)]
    mine, other = refs[sum(counts):][:groups], refs[sum(counts) + groups:][:groups]
    out_ref, dressed = refs[-2:]
    first = flags[0] == 0
    at = 0
    for m, o in zip(mine, other):
        rows = m.shape[0]
        dressed[at:at + rows, :] = joined(first, m[...], o[...])
        at += rows
    vir = t_ref.shape[2]
    step = 256 if vir % 256 == 0 else vir
    for k in range(t_ref.shape[0]):
        for start in range(0, vir, step):
            cols = slice(start, start + step)
            total = jnp.dot(t_ref[k, cols, :], fock_ref[...], preferred_element_type=jnp.float32)
            left = jnp.concatenate([c[k, :, cols] for c in chunks], axis=0)
            total += lax.dot_general(
                left, dressed[...], (((0,), (0,)), ((), ())), preferred_element_type=jnp.float32
            )
            out_ref[k, cols, :] = total


def numer(flags, t, fock, chunk_groups, mine, other):
    chunks = [c for group in chunk_groups for c in group]
    rows = sum(c.shape[1] for c in chunks)
    occ, vir = t.shape[0], t.shape[2]
    vmem = pl.BlockSpec(memory_space=pltpu.VMEM)
    return pl.pallas_call(
        functools.partial(numer_kernel, [len(group) for group in chunk_groups]),
        out_shape=jax.ShapeDtypeStruct((occ, vir, vir), jnp.float32),
        in_specs=[pl.BlockSpec(memory_space=pltpu.SMEM)]
        + [vmem] * (2 + len(chunks) + len(mine) + len(other)),
        out_specs=vmem,
        scratch_shapes=[pltpu.VMEM((rows, vir), jnp.bfloat16)],
        compiler_params=pltpu.CompilerParams(vmem_limit_bytes=VMEM_LIMIT),
        cost_estimate=pl.CostEstimate(
            flops=2 * occ * vir * vir * (rows + vir),
            bytes_accessed=2 * rows * vir * (occ + 1) + 6 * t.size,
            transcendentals=0,
        ),
        name="numer",
    )(flags, t, fock, *chunks, *mine, *other)


def turn_kernel(*refs):
    out_ref = refs[-1]
    for k in range(out_ref.shape[0]):
        out_ref[k] = jnp.concatenate([c[k] for c in refs[:-1]], axis=0).T


def turn(chunks):
    rows = sum(c.shape[1] for c in chunks)
    occ, _, vir = chunks[0].shape
    vmem = pl.BlockSpec(memory_space=pltpu.VMEM)
    return pl.pallas_call(
        turn_kernel,
        out_shape=jax.ShapeDtypeStruct((occ, vir, rows), jnp.bfloat16),
        in_specs=[vmem] * len(chunks),
        out_specs=vmem,
        compiler_params=pltpu.CompilerParams(vmem_limit_bytes=VMEM_LIMIT),
        cost_estimate=pl.CostEstimate(
            flops=0, bytes_accessed=4 * occ * vir * rows, transcendentals=0
        ),
        name="turn",
    )(*chunks)


def final_kernel(flags, eps_first, acc_ref, left_ref, t_ref, mine, other, rows_ref, cols_ref, out_ref):
    dressed = joined(flags[0] == 0, mine[...], other[...])
    total = acc_ref[0] + jnp.dot(left_ref[0], dressed, preferred_element_type=jnp.float32)
    denom = (rows_ref[...] - eps_first[pl.program_id(0)]) + cols_ref[...]
    out_ref[0, 0] = (t_ref[0, 0].astype(jnp.float32) - total / denom).astype(out_ref.dtype)


def final(flags, eps_first, acc, left, t, mine, other, eps_rows, eps_cols):
    occ, vir, rows = left.shape
    step = 256 if vir % 256 == 0 else vir
    smem = pl.BlockSpec(memory_space=pltpu.SMEM)
    return pl.pallas_call(
        final_kernel,
        grid=(occ, vir // step),
        out_shape=jax.ShapeDtypeStruct(t.shape, t.dtype),
        in_specs=[
            smem,
            smem,
            pl.BlockSpec((1, step, vir), lambda k, a: (k, a, 0)),
            pl.BlockSpec((1, step, rows), lambda k, a: (k, a, 0)),
            pl.BlockSpec((1, 1, step, vir), lambda k, a: (k, 0, a, 0)),
            pl.BlockSpec(mine.shape, lambda k, a: (0, 0)),
            pl.BlockSpec(other.shape, lambda k, a: (0, 0)),
            pl.BlockSpec((step, 1), lambda k, a: (a, 0)),
            pl.BlockSpec((1, vir), lambda k, a: (0, 0)),
        ],
        out_specs=pl.BlockSpec((1, 1, step, vir), lambda k, a: (k, 0, a, 0)),
        compiler_params=pltpu.CompilerParams(vmem_limit_bytes=VMEM_LIMIT),
        cost_estimate=pl.CostEstimate(
            flops=2 * occ * vir * vir * rows, bytes_accessed=8 * t.size, transcendentals=0
        ),
        name="final",
    )(flags, eps_first, acc, left, t, mine, other, eps_rows, eps_cols)


def local(n_row, n_col, amplitudes, ints, eps_occ, eps_vir, fock_vir):
    occ, _, vir, _ = amplitudes.shape
    row, col = lax.axis_index("row"), lax.axis_index("col")
    t = amplitudes[:, 0]
    shard = jnp.swapaxes(ints, 1, 2)
    q = shard.shape[1]
    cut = (q // 2 + 15) // 16 * 16

    order = ring_order(n_col)
    up = [(order[p], order[(p + 1) % n_col]) for p in range(n_col)]
    down = [(b, a) for a, b in up]

    own = [shard[:, :cut], shard[:, cut:]]
    steps = []
    ups, downs = list(own), list(own)
    for step in range(n_col - 2):
        h = step % 2
        ups[h] = lax.ppermute(ups[h], "col", up)
        downs[h] = lax.ppermute(downs[h], "col", down)
        steps.append([ups[h], downs[h]])
    steps.append([lax.ppermute(ups[0], "col", up), lax.ppermute(downs[1], "col", down)])

    groups = []
    at = 0
    for size in group_sizes(len(steps)):
        groups.append([c for pair in steps[at:at + size] for c in pair])
        at += size
    groups[0] = own + groups[0]

    core = row % 2
    first_ids = row * occ + jnp.arange(occ, dtype=jnp.int32)
    flags = jnp.concatenate(
        [core[None].astype(jnp.int32), (first_ids == col).astype(jnp.int32)]
    )

    def swap(x, bit):
        return lax.ppermute(x, "row", [(r, r ^ bit) for r in range(n_row)])

    mine, other = [], []
    for group in groups:
        total, send = cross(flags, t, group)
        total = total + swap(send, 1).astype(jnp.float32)
        bit = 2
        while bit < n_row:
            total = total + swap(total.astype(jnp.bfloat16), bit).astype(jnp.float32)
            bit *= 2
        mine.append(total.astype(jnp.bfloat16))
        other.append(swap(mine[-1], 1))

    acc = numer(flags, t, fock_vir, groups[:-1], mine[:-1], other[:-1])
    left = turn(groups[-1])
    eps_first = lax.dynamic_slice_in_dim(eps_occ, row * occ, occ, 0)
    eps_second = lax.dynamic_slice_in_dim(eps_occ, col, 1, 0)
    eps_rows = (eps_vir - eps_second)[:, None]
    return final(
        flags, eps_first, acc, left, amplitudes, mine[-1], other[-1], eps_rows, eps_vir[None, :]
    )


def solution(mesh):
    placed = (P("row", "col", None, None), P("row", None, "col"), P(), P(), P())
    body = functools.partial(local, mesh.shape["row"], mesh.shape["col"])
    return jax.shard_map(
        body, mesh=mesh, in_specs=placed, out_specs=P("row", "col", None, None), check_vma=False
    )
```

```python
import functools

import jax
import jax.numpy as jnp
from jax import lax
from jax.experimental import pallas as pl
from jax.experimental.pallas import tpu as pltpu
from jax.sharding import PartitionSpec as P

MIB = 1024 * 1024
VMEM = pl.BlockSpec(memory_space=pltpu.VMEM)
SMEM = pl.BlockSpec(memory_space=pltpu.SMEM)


def cost(flops, moved):
    return pl.CostEstimate(
        flops=flops // 1000 + 1, bytes_accessed=moved // 1000 + 1, transcendentals=0
    )


def ring_order(n):
    low = max(d for d in range(1, n + 1) if n % d == 0 and d * d <= n)
    high = n // low
    if low == 1 or high % 2:
        return list(range(n))
    order = [h * low for h in range(high)]
    for turn, h in enumerate(reversed(range(high))):
        lows = range(1, low) if turn % 2 == 0 else range(low - 1, 0, -1)
        order += [h * low + l for l in lows]
    return order


def after(values, gate):
    return lax.optimization_barrier((values, gate))[0]


def cross_kernel(flags, t_ref, *refs):
    chunks, (keep_ref, send_ref) = refs[:-2], refs[-2:]
    occ, vir = t_ref.shape[0], t_ref.shape[2]
    half = vir // 2
    first = flags[0] == 0
    at = 0
    for c in chunks:
        total = None
        for k in range(occ):
            part = jnp.dot(c[k], t_ref[k], preferred_element_type=jnp.float32)
            part = part + jnp.where(flags[2 + k] == 1, c[k].astype(jnp.float32), 0.0)
            total = part if total is None else total + part
        low, high = total[:, :half], total[:, half:]
        rows = slice(at, at + c.shape[1])
        keep_ref[rows, :] = jnp.where(first, low, high)
        send_ref[rows, :] = jnp.where(first, high, low).astype(send_ref.dtype)
        at += c.shape[1]


def cross(flags, t, chunks):
    rows = sum(c.shape[1] for c in chunks)
    occ, _, vir = t.shape
    return pl.pallas_call(
        cross_kernel,
        out_shape=(
            jax.ShapeDtypeStruct((rows, vir // 2), jnp.float32),
            jax.ShapeDtypeStruct((rows, vir // 2), jnp.bfloat16),
        ),
        in_specs=[SMEM] + [VMEM] * (1 + len(chunks)),
        out_specs=(VMEM, VMEM),
        compiler_params=pltpu.CompilerParams(vmem_limit_bytes=20 * MIB),
        cost_estimate=cost(2 * rows * vir * vir * occ, 2 * t.size + 2 * rows * vir * (occ + 2)),
        name="cross",
    )(flags, t, *chunks)


def dressed_rows(flags, mine, other):
    first = flags[0] == 0
    return jnp.concatenate(
        [jnp.where(first, mine, other), jnp.where(first, other, mine)], axis=1
    )


def tiles(vir):
    step = 256 if vir % 256 == 0 else vir
    return [slice(start, start + step) for start in range(0, vir, step)]


def pair_product(chunks, dressed, k, cols):
    left = jnp.concatenate([c[k, :, cols] for c in chunks], axis=0)
    return lax.dot_general(
        left, dressed, (((0,), (0,)), ((), ())), preferred_element_type=jnp.float32
    )


def numer_kernel(n_chunks, n_groups, fresh, flags, *refs):
    refs = list(refs)
    lead = [refs.pop(0) for _ in range(2 if fresh else 1)]
    chunks = [refs.pop(0) for _ in range(n_chunks)]
    mine = [refs.pop(0) for _ in range(n_groups)]
    other = [refs.pop(0) for _ in range(n_groups)]
    out_ref, dressed = refs
    at = 0
    for m, o in zip(mine, other):
        dressed[at:at + m.shape[0], :] = dressed_rows(flags, m[...], o[...])
        at += m.shape[0]
    occ, vir = out_ref.shape[:2]
    for k in range(occ):
        for cols in tiles(vir):
            if fresh:
                total = jnp.dot(
                    lead[0][k, cols, :], lead[1][...], preferred_element_type=jnp.float32
                )
            else:
                total = lead[0][k, cols, :]
            out_ref[k, cols, :] = total + pair_product(chunks, dressed[...], k, cols)


def numer(flags, lead, chunk_groups, mine, other):
    fresh = len(lead) == 2
    chunks = [c for group in chunk_groups for c in group]
    rows = sum(c.shape[1] for c in chunks)
    occ, vir = lead[0].shape[:2]
    operands = [flags, *lead, *chunks, *mine, *other]
    return pl.pallas_call(
        functools.partial(numer_kernel, len(chunks), len(mine), fresh),
        out_shape=jax.ShapeDtypeStruct((occ, vir, vir), jnp.float32),
        in_specs=[SMEM] + [VMEM] * (len(operands) - 1),
        out_specs=VMEM,
        input_output_aliases={} if fresh else {1: 0},
        scratch_shapes=[pltpu.VMEM((rows, vir), jnp.bfloat16)],
        compiler_params=pltpu.CompilerParams(vmem_limit_bytes=30 * MIB),
        cost_estimate=cost(
            2 * occ * vir * vir * (rows + vir * fresh),
            2 * rows * vir * (occ + 1) + 6 * occ * vir * vir,
        ),
        name="numer",
    )(*operands)


def final_kernel(n_chunks, n_groups, flags, eps_occ, acc_ref, t_ref, eps_row, eps_col, *refs):
    refs = list(refs)
    chunks = [refs.pop(0) for _ in range(n_chunks)]
    mine = [refs.pop(0) for _ in range(n_groups)]
    other = [refs.pop(0) for _ in range(n_groups)]
    out_ref, dressed, tile, sems = refs
    at = 0
    for m, o in zip(mine, other):
        dressed[at:at + m.shape[0], :] = dressed_rows(flags, m[...], o[...])
        at += m.shape[0]
    occ, vir = acc_ref.shape[:2]
    second = eps_occ[flags[1]]
    copies = []
    for k in range(occ):
        first = eps_occ[flags[2 + occ] + k]
        for n, cols in enumerate(tiles(vir)):
            total = acc_ref[k, cols, :] + pair_product(chunks, dressed[...], k, cols)
            denom = (eps_col[cols, :] - first) + (eps_row[...] - second)
            new = t_ref[k, cols, :].astype(jnp.float32) - total / denom
            tile[k, cols, :] = new.astype(tile.dtype)
            copy = pltpu.make_async_copy(
                tile.at[k, cols, :], out_ref.at[k, 0, cols, :], sems.at[k, n]
            )
            copy.start()
            copies.append(copy)
    for copy in copies:
        copy.wait()


def final(flags, eps_occ, acc, t, eps_vir, chunk_groups, mine, other):
    occ, vir = acc.shape[:2]
    chunks = [c for group in chunk_groups for c in group]
    rows = sum(c.shape[1] for c in chunks)
    operands = [flags, eps_occ, acc, t, eps_vir[None, :], eps_vir[:, None], *chunks, *mine, *other]
    return pl.pallas_call(
        functools.partial(final_kernel, len(chunks), len(mine)),
        out_shape=jax.ShapeDtypeStruct((occ, 1, vir, vir), t.dtype),
        in_specs=[SMEM, SMEM] + [VMEM] * (len(operands) - 2),
        out_specs=pl.BlockSpec(memory_space=pl.ANY),
        scratch_shapes=[
            pltpu.VMEM((rows, vir), t.dtype),
            pltpu.VMEM((occ, vir, vir), t.dtype),
            pltpu.SemaphoreType.DMA((occ, len(tiles(vir)))),
        ],
        compiler_params=pltpu.CompilerParams(vmem_limit_bytes=24 * MIB),
        cost_estimate=cost(2 * occ * vir * vir * rows, 8 * t.size),
        name="final",
    )(*operands)


def local(n_row, n_col, amplitudes, ints, eps_occ, eps_vir, fock_vir):
    occ = amplitudes.shape[0]
    row, col = lax.axis_index("row"), lax.axis_index("col")
    t = amplitudes[:, 0]
    shard = jnp.swapaxes(ints, 1, 2)
    q = shard.shape[1]
    cut = (q // 2 + 15) // 16 * 16

    order = ring_order(n_col)
    up = [(order[p], order[(p + 1) % n_col]) for p in range(n_col)]
    down = [(b, a) for a, b in up]

    first_ids = row * occ + jnp.arange(occ, dtype=jnp.int32)
    flags = jnp.concatenate(
        [
            jnp.stack([row % 2, col]).astype(jnp.int32),
            (first_ids == col).astype(jnp.int32),
            first_ids[:1],
        ]
    )

    def swap(x, bit):
        return lax.ppermute(x, "row", [(r, r ^ bit) for r in range(n_row)])

    last = n_col - 1
    own = [shard[:, :cut], shard[:, cut:]]
    ups, downs = list(own), list(own)
    vals = {}
    pairs = last - 3
    sizes = [1] + [2] * (pairs // 2) + [1] * (pairs % 2) + [1, 1]
    ng = len(sizes)
    ends = [sum(sizes[:n + 1]) for n in range(ng)]
    ties = {}
    for n, end in enumerate(ends[:-1]):
        z_at = "R%d" % (end + 4) if end + 4 <= last else "C%d" % (n + 1)
        ties.setdefault(z_at, []).append("Z%d" % n)
        if n < ng - 3:
            w_at = "R%d" % (end + 6) if end + 6 <= last else "C%d" % (ng - 1)
            ties.setdefault(w_at, []).append("W%d" % n)

    def tie(value, target):
        src = [vals[x] for x in ties.get(target, [])]
        return after(value, src) if src else value

    def ring_step(step):
        h = (step - 1) % 2
        up_h, down_h = (0, 1) if step == last else (h, 1 - h)
        ups[up_h], downs[down_h] = tie((ups[up_h], downs[down_h]), "R%d" % step)
        ups[up_h] = lax.ppermute(ups[up_h], "col", up)
        downs[down_h] = lax.ppermute(downs[down_h], "col", down)
        return [ups[up_h], downs[down_h]]

    groups, mine, other = [], [], []
    n0, n1 = max(ng - 4, 1), ng - 2
    numer_at = {"C%d" % (ng - 1): "N0", "G%d" % (ng - 1): "N1"}

    def through(value, target):
        name = numer_at.get(target)
        if name == "N0":
            vals[name] = numer(flags, (t, fock_vir), groups[:n0], mine[:n0], other[:n0])
        elif name == "N1":
            vals[name] = numer(flags, (vals["N0"],), groups[n0:n1], mine[n0:n1], other[n0:n1])
        if name:
            value, vals[name] = lax.optimization_barrier((value, vals[name]))
        return tie(value, target)

    group, g = list(own), 0
    for step in range(1, last + 1):
        group = group + ring_step(step)
        if step not in ends:
            continue
        group = through(group, "C%d" % g)
        total, send = cross(flags, t, group)
        total = total + swap(send, 1).astype(jnp.float32)
        bit = 2
        while bit < n_row:
            send = total.astype(jnp.bfloat16)
            vals["Z%d" % g] = send
            got = through(swap(send, bit), "G%d" % g)
            total = total + got.astype(jnp.float32)
            bit *= 2
        groups.append(group)
        total = total.astype(jnp.bfloat16)
        vals["W%d" % g] = total
        mine.append(total)
        other.append(swap(total, 1))
        group = []
        g += 1
    acc = vals["N1"]
    return final(flags, eps_occ, acc, t, eps_vir, groups[n1:], mine[n1:], other[n1:])


def solution(mesh):
    placed = (P("row", "col", None, None), P("row", None, "col"), P(), P(), P())
    body = functools.partial(local, mesh.shape["row"], mesh.shape["col"])
    return jax.shard_map(
        body, mesh=mesh, in_specs=placed, out_specs=P("row", "col", None, None), check_vma=False
    )
```

```python
import functools

import jax
import jax.numpy as jnp
from jax import lax
from jax.experimental import pallas as pl
from jax.experimental.pallas import tpu as pltpu
from jax.sharding import PartitionSpec as P

MIB = 1024 * 1024
VMEM = pl.BlockSpec(memory_space=pltpu.VMEM)
SMEM = pl.BlockSpec(memory_space=pltpu.SMEM)


def cost(flops, moved):
    return pl.CostEstimate(
        flops=flops // 1000 + 1, bytes_accessed=moved // 1000 + 1, transcendentals=0
    )


def ring_order(n):
    low = max(d for d in range(1, n + 1) if n % d == 0 and d * d <= n)
    high = n // low
    if low == 1 or high % 2:
        return list(range(n))
    order = [h * low for h in range(high)]
    for turn, h in enumerate(reversed(range(high))):
        lows = range(1, low) if turn % 2 == 0 else range(low - 1, 0, -1)
        order += [h * low + l for l in lows]
    return order


def after(values, gate):
    return lax.optimization_barrier((values, gate))[0]


def cross_kernel(flags, t_ref, *refs):
    chunks, (keep_ref, send_ref) = refs[:-2], refs[-2:]
    occ, vir = t_ref.shape[0], t_ref.shape[2]
    half = vir // 2
    first = flags[0] == 0
    at = 0
    for c in chunks:
        total = None
        for k in range(occ):
            part = jnp.dot(c[k], t_ref[k], preferred_element_type=jnp.float32)
            part = part + jnp.where(flags[2 + k] == 1, c[k].astype(jnp.float32), 0.0)
            total = part if total is None else total + part
        low, high = total[:, :half], total[:, half:]
        rows = slice(at, at + c.shape[1])
        keep_ref[rows, :] = jnp.where(first, low, high)
        send_ref[rows, :] = jnp.where(first, high, low).astype(send_ref.dtype)
        at += c.shape[1]


def cross(flags, t, chunks):
    rows = sum(c.shape[1] for c in chunks)
    occ, _, vir = t.shape
    return pl.pallas_call(
        cross_kernel,
        out_shape=(
            jax.ShapeDtypeStruct((rows, vir // 2), jnp.float32),
            jax.ShapeDtypeStruct((rows, vir // 2), jnp.bfloat16),
        ),
        in_specs=[SMEM] + [VMEM] * (1 + len(chunks)),
        out_specs=(VMEM, VMEM),
        compiler_params=pltpu.CompilerParams(vmem_limit_bytes=20 * MIB),
        cost_estimate=cost(2 * rows * vir * vir * occ, 2 * t.size + 2 * rows * vir * (occ + 2)),
        name="cross",
    )(flags, t, *chunks)


def dressed_rows(flags, mine, other):
    first = flags[0] == 0
    return jnp.concatenate(
        [jnp.where(first, mine, other), jnp.where(first, other, mine)], axis=1
    )


def tiles(vir):
    step = 256 if vir % 256 == 0 else vir
    return [slice(start, start + step) for start in range(0, vir, step)]


def pair_product(chunks, dressed, k, cols):
    left = jnp.concatenate([c[k, :, cols] for c in chunks], axis=0)
    return lax.dot_general(
        left, dressed, (((0,), (0,)), ((), ())), preferred_element_type=jnp.float32
    )


def numer_kernel(n_chunks, n_groups, fresh, flags, *refs):
    refs = list(refs)
    lead = [refs.pop(0) for _ in range(2 if fresh else 1)]
    chunks = [refs.pop(0) for _ in range(n_chunks)]
    mine = [refs.pop(0) for _ in range(n_groups)]
    other = [refs.pop(0) for _ in range(n_groups)]
    out_ref, dressed = refs
    at = 0
    for m, o in zip(mine, other):
        dressed[at:at + m.shape[0], :] = dressed_rows(flags, m[...], o[...])
        at += m.shape[0]
    occ, vir = out_ref.shape[:2]
    for k in range(occ):
        for cols in tiles(vir):
            if fresh:
                total = jnp.dot(
                    lead[0][k, cols, :], lead[1][...], preferred_element_type=jnp.float32
                )
            else:
                total = lead[0][k, cols, :]
            out_ref[k, cols, :] = total + pair_product(chunks, dressed[...], k, cols)


def numer(flags, lead, chunk_groups, mine, other):
    fresh = len(lead) == 2
    chunks = [c for group in chunk_groups for c in group]
    rows = sum(c.shape[1] for c in chunks)
    occ, vir = lead[0].shape[:2]
    operands = [flags, *lead, *chunks, *mine, *other]
    return pl.pallas_call(
        functools.partial(numer_kernel, len(chunks), len(mine), fresh),
        out_shape=jax.ShapeDtypeStruct((occ, vir, vir), jnp.float32),
        in_specs=[SMEM] + [VMEM] * (len(operands) - 1),
        out_specs=VMEM,
        input_output_aliases={} if fresh else {1: 0},
        scratch_shapes=[pltpu.VMEM((rows, vir), jnp.bfloat16)],
        compiler_params=pltpu.CompilerParams(vmem_limit_bytes=30 * MIB),
        cost_estimate=cost(
            2 * occ * vir * vir * (rows + vir * fresh),
            2 * rows * vir * (occ + 1) + 6 * occ * vir * vir,
        ),
        name="numer",
    )(*operands)


def final_kernel(n_chunks, n_groups, flags, eps_occ, acc_ref, t_ref, eps_row, eps_col, *refs):
    refs = list(refs)
    chunks = [refs.pop(0) for _ in range(n_chunks)]
    mine = [refs.pop(0) for _ in range(n_groups)]
    other = [refs.pop(0) for _ in range(n_groups)]
    out_ref, dressed, tile, sems = refs
    at = 0
    for m, o in zip(mine, other):
        dressed[at:at + m.shape[0], :] = dressed_rows(flags, m[...], o[...])
        at += m.shape[0]
    occ, vir = acc_ref.shape[:2]
    second = eps_occ[flags[1]]
    copies = []
    for k in range(occ):
        first = eps_occ[flags[2 + occ] + k]
        for n, cols in enumerate(tiles(vir)):
            total = acc_ref[k, cols, :] + pair_product(chunks, dressed[...], k, cols)
            denom = (eps_col[cols, :] - first) + (eps_row[...] - second)
            inverse = pl.reciprocal(denom, approx=True)
            inverse = inverse * (2.0 - denom * inverse)
            new = t_ref[k, cols, :].astype(jnp.float32) - total * inverse
            tile[k, cols, :] = new.astype(tile.dtype)
            copy = pltpu.make_async_copy(
                tile.at[k, cols, :], out_ref.at[k, 0, cols, :], sems.at[k, n]
            )
            copy.start()
            copies.append(copy)
    for copy in copies:
        copy.wait()


def final(flags, eps_occ, acc, t, eps_vir, chunk_groups, mine, other):
    occ, vir = acc.shape[:2]
    chunks = [c for group in chunk_groups for c in group]
    rows = sum(c.shape[1] for c in chunks)
    operands = [flags, eps_occ, acc, t, eps_vir[None, :], eps_vir[:, None], *chunks, *mine, *other]
    return pl.pallas_call(
        functools.partial(final_kernel, len(chunks), len(mine)),
        out_shape=jax.ShapeDtypeStruct((occ, 1, vir, vir), t.dtype),
        in_specs=[SMEM, SMEM] + [VMEM] * (len(operands) - 2),
        out_specs=pl.BlockSpec(memory_space=pl.ANY),
        scratch_shapes=[
            pltpu.VMEM((rows, vir), t.dtype),
            pltpu.VMEM((occ, vir, vir), t.dtype),
            pltpu.SemaphoreType.DMA((occ, len(tiles(vir)))),
        ],
        compiler_params=pltpu.CompilerParams(vmem_limit_bytes=24 * MIB),
        cost_estimate=cost(2 * occ * vir * vir * rows, 8 * t.size),
        name="final",
    )(*operands)


def local(n_row, n_col, amplitudes, ints, eps_occ, eps_vir, fock_vir):
    occ = amplitudes.shape[0]
    row, col = lax.axis_index("row"), lax.axis_index("col")
    t = amplitudes[:, 0]
    shard = jnp.swapaxes(ints, 1, 2)
    q = shard.shape[1]
    cut = (q // 2 + 15) // 16 * 16

    order = ring_order(n_col)
    up = [(order[p], order[(p + 1) % n_col]) for p in range(n_col)]
    down = [(b, a) for a, b in up]

    first_ids = row * occ + jnp.arange(occ, dtype=jnp.int32)
    flags = jnp.concatenate(
        [
            jnp.stack([row % 2, col]).astype(jnp.int32),
            (first_ids == col).astype(jnp.int32),
            first_ids[:1],
        ]
    )

    def swap(x, bit):
        return lax.ppermute(x, "row", [(r, r ^ bit) for r in range(n_row)])

    last = n_col - 1
    own = [shard[:, :cut], shard[:, cut:]]
    ups, downs = list(own), list(own)
    vals = {}
    pairs = last - 3
    sizes = [1] + [2] * (pairs // 2) + [1] * (pairs % 2) + [1, 1]
    ng = len(sizes)
    ends = [sum(sizes[:n + 1]) for n in range(ng)]
    ties = {}
    for n, end in enumerate(ends[:-1]):
        if n != ng - 3:
            z_at = "R%d" % (end + 4) if end + 4 <= last else "C%d" % (n + 1)
            ties.setdefault(z_at, []).append("Z%d" % n)
        if n < ng - 3:
            w_at = "R%d" % (end + 6) if end + 6 <= last else "C%d" % (ng - 1)
            ties.setdefault(w_at, []).append("W%d" % n)

    def tie(value, target):
        src = [vals[x] for x in ties.get(target, [])]
        return after(value, src) if src else value

    def ring_step(step):
        h = (step - 1) % 2
        up_h, down_h = (0, 1) if step == last else (h, 1 - h)
        ups[up_h], downs[down_h] = tie((ups[up_h], downs[down_h]), "R%d" % step)
        ups[up_h] = lax.ppermute(ups[up_h], "col", up)
        downs[down_h] = lax.ppermute(downs[down_h], "col", down)
        return [ups[up_h], downs[down_h]]

    groups, mine, other = [], [], []
    n0, n1 = ng - 3, ng - 2
    numer_at = {"C%d" % (ng - 1): "N0", "G%d" % (ng - 1): "N1"}

    def through(value, target):
        name = numer_at.get(target)
        if name == "N0":
            vals[name] = numer(flags, (t, fock_vir), groups[:n0], mine[:n0], other[:n0])
        elif name == "N1":
            vals[name] = numer(flags, (vals["N0"],), groups[n0:n1], mine[n0:n1], other[n0:n1])
        if name:
            value, vals[name] = lax.optimization_barrier((value, vals[name]))
        return tie(value, target)

    group, g = list(own), 0
    for step in range(1, last + 1):
        group = group + ring_step(step)
        if step not in ends:
            continue
        group = through(group, "C%d" % g)
        total, send = cross(flags, t, group)
        total = total + swap(send, 1).astype(jnp.float32)
        bit = 2
        while bit < n_row:
            send = total.astype(jnp.bfloat16)
            vals["Z%d" % g] = send
            got = through(swap(send, bit), "G%d" % g)
            total = total + got.astype(jnp.float32)
            bit *= 2
        groups.append(group)
        total = total.astype(jnp.bfloat16)
        vals["W%d" % g] = total
        mine.append(total)
        other.append(swap(total, 1))
        group = []
        g += 1
    acc = vals["N1"]
    return final(flags, eps_occ, acc, t, eps_vir, groups[n1:], mine[n1:], other[n1:])


def solution(mesh):
    placed = (P("row", "col", None, None), P("row", None, "col"), P(), P(), P())
    body = functools.partial(local, mesh.shape["row"], mesh.shape["col"])
    return jax.shard_map(
        body, mesh=mesh, in_specs=placed, out_specs=P("row", "col", None, None), check_vma=False
    )
```

```python
import functools

import jax
import jax.numpy as jnp
from jax import lax
from jax.experimental import pallas as pl
from jax.experimental.pallas import tpu as pltpu
from jax.sharding import PartitionSpec as P

MIB = 1024 * 1024
VMEM = pl.BlockSpec(memory_space=pltpu.VMEM)
SMEM = pl.BlockSpec(memory_space=pltpu.SMEM)


def cost(flops, moved):
    return pl.CostEstimate(
        flops=flops // 1000 + 1, bytes_accessed=moved // 1000 + 1, transcendentals=0
    )


def ring_order(n):
    low = max(d for d in range(1, n + 1) if n % d == 0 and d * d <= n)
    high = n // low
    if low == 1 or high % 2:
        return list(range(n))
    order = [h * low for h in range(high)]
    for turn, h in enumerate(reversed(range(high))):
        lows = range(1, low) if turn % 2 == 0 else range(low - 1, 0, -1)
        order += [h * low + l for l in lows]
    return order


def after(values, gate):
    return lax.optimization_barrier((values, gate))[0]


def cross_kernel(flags, t_ref, *refs):
    chunks, (keep_ref, send_ref) = refs[:-2], refs[-2:]
    occ, vir = t_ref.shape[0], t_ref.shape[2]
    half = vir // 2
    first = flags[0] == 0
    at = 0
    for c in chunks:
        total = None
        for k in range(occ):
            part = jnp.dot(c[k], t_ref[k], preferred_element_type=jnp.float32)
            part = part + jnp.where(flags[2 + k] == 1, c[k].astype(jnp.float32), 0.0)
            total = part if total is None else total + part
        low, high = total[:, :half], total[:, half:]
        rows = slice(at, at + c.shape[1])
        keep_ref[rows, :] = jnp.where(first, low, high)
        send_ref[rows, :] = jnp.where(first, high, low).astype(send_ref.dtype)
        at += c.shape[1]


def cross(flags, t, chunks):
    rows = sum(c.shape[1] for c in chunks)
    occ, _, vir = t.shape
    return pl.pallas_call(
        cross_kernel,
        out_shape=(
            jax.ShapeDtypeStruct((rows, vir // 2), jnp.float32),
            jax.ShapeDtypeStruct((rows, vir // 2), jnp.bfloat16),
        ),
        in_specs=[SMEM] + [VMEM] * (1 + len(chunks)),
        out_specs=(VMEM, VMEM),
        compiler_params=pltpu.CompilerParams(vmem_limit_bytes=20 * MIB),
        cost_estimate=cost(2 * rows * vir * vir * occ, 2 * t.size + 2 * rows * vir * (occ + 2)),
        name="cross",
    )(flags, t, *chunks)


def dressed_rows(flags, mine, other):
    first = flags[0] == 0
    return jnp.concatenate(
        [jnp.where(first, mine, other), jnp.where(first, other, mine)], axis=1
    )


def tiles(vir):
    step = 256 if vir % 256 == 0 else vir
    return [slice(start, start + step) for start in range(0, vir, step)]


def pair_product(chunks, dressed, k, cols):
    left = jnp.concatenate([c[k, :, cols] for c in chunks], axis=0)
    return lax.dot_general(
        left, dressed, (((0,), (0,)), ((), ())), preferred_element_type=jnp.float32
    )


def numer_kernel(n_chunks, n_groups, fresh, flags, *refs):
    refs = list(refs)
    lead = [refs.pop(0) for _ in range(2 if fresh else 1)]
    chunks = [refs.pop(0) for _ in range(n_chunks)]
    mine = [refs.pop(0) for _ in range(n_groups)]
    other = [refs.pop(0) for _ in range(n_groups)]
    out_ref, dressed = refs
    at = 0
    for m, o in zip(mine, other):
        dressed[at:at + m.shape[0], :] = dressed_rows(flags, m[...], o[...])
        at += m.shape[0]
    occ, vir = out_ref.shape[:2]
    for k in range(occ):
        for cols in tiles(vir):
            if fresh:
                total = jnp.dot(
                    lead[0][k, cols, :], lead[1][...], preferred_element_type=jnp.float32
                )
            else:
                total = lead[0][k, cols, :]
            out_ref[k, cols, :] = total + pair_product(chunks, dressed[...], k, cols)


def numer(flags, lead, chunk_groups, mine, other):
    fresh = len(lead) == 2
    chunks = [c for group in chunk_groups for c in group]
    rows = sum(c.shape[1] for c in chunks)
    occ, vir = lead[0].shape[:2]
    operands = [flags, *lead, *chunks, *mine, *other]
    return pl.pallas_call(
        functools.partial(numer_kernel, len(chunks), len(mine), fresh),
        out_shape=jax.ShapeDtypeStruct((occ, vir, vir), jnp.float32),
        in_specs=[SMEM] + [VMEM] * (len(operands) - 1),
        out_specs=VMEM,
        input_output_aliases={} if fresh else {1: 0},
        scratch_shapes=[pltpu.VMEM((rows, vir), jnp.bfloat16)],
        compiler_params=pltpu.CompilerParams(vmem_limit_bytes=30 * MIB),
        cost_estimate=cost(
            2 * occ * vir * vir * (rows + vir * fresh),
            2 * rows * vir * (occ + 1) + 6 * occ * vir * vir,
        ),
        name="numer",
    )(*operands)


def final_kernel(n_chunks, n_groups, flags, eps_occ, acc_ref, t_ref, eps_row, eps_col, *refs):
    refs = list(refs)
    chunks = [refs.pop(0) for _ in range(n_chunks)]
    mine = [refs.pop(0) for _ in range(n_groups)]
    other = [refs.pop(0) for _ in range(n_groups)]
    out_ref, dressed, tile, sems = refs
    at = 0
    for m, o in zip(mine, other):
        dressed[at:at + m.shape[0], :] = dressed_rows(flags, m[...], o[...])
        at += m.shape[0]
    occ, vir = acc_ref.shape[:2]
    second = eps_occ[flags[1]]
    copies = []
    for k in range(occ):
        first = eps_occ[flags[2 + occ] + k]
        for n, cols in enumerate(tiles(vir)):
            total = acc_ref[k, cols, :] + pair_product(chunks, dressed[...], k, cols)
            denom = (eps_col[cols, :] - first) + (eps_row[...] - second)
            new = t_ref[k, cols, :].astype(jnp.float32) - total / denom
            tile[k, cols, :] = new.astype(tile.dtype)
            copy = pltpu.make_async_copy(
                tile.at[k, cols, :], out_ref.at[k, 0, cols, :], sems.at[k, n]
            )
            copy.start()
            copies.append(copy)
    for copy in copies:
        copy.wait()


def final(flags, eps_occ, acc, t, eps_vir, chunk_groups, mine, other):
    occ, vir = acc.shape[:2]
    chunks = [c for group in chunk_groups for c in group]
    rows = sum(c.shape[1] for c in chunks)
    operands = [flags, eps_occ, acc, t, eps_vir[None, :], eps_vir[:, None], *chunks, *mine, *other]
    return pl.pallas_call(
        functools.partial(final_kernel, len(chunks), len(mine)),
        out_shape=jax.ShapeDtypeStruct((occ, 1, vir, vir), t.dtype),
        in_specs=[SMEM, SMEM] + [VMEM] * (len(operands) - 2),
        out_specs=pl.BlockSpec(memory_space=pl.ANY),
        scratch_shapes=[
            pltpu.VMEM((rows, vir), t.dtype),
            pltpu.VMEM((occ, vir, vir), t.dtype),
            pltpu.SemaphoreType.DMA((occ, len(tiles(vir)))),
        ],
        compiler_params=pltpu.CompilerParams(vmem_limit_bytes=24 * MIB),
        cost_estimate=cost(2 * occ * vir * vir * rows, 8 * t.size),
        name="final",
    )(*operands)


def local(n_row, n_col, amplitudes, ints, eps_occ, eps_vir, fock_vir):
    occ = amplitudes.shape[0]
    row, col = lax.axis_index("row"), lax.axis_index("col")
    t = amplitudes[:, 0]
    shard = jnp.swapaxes(ints, 1, 2)
    q = shard.shape[1]
    cut = (q // 2 + 15) // 16 * 16

    order = ring_order(n_col)
    up = [(order[p], order[(p + 1) % n_col]) for p in range(n_col)]
    down = [(b, a) for a, b in up]

    first_ids = row * occ + jnp.arange(occ, dtype=jnp.int32)
    flags = jnp.concatenate(
        [
            jnp.stack([row % 2, col]).astype(jnp.int32),
            (first_ids == col).astype(jnp.int32),
            first_ids[:1],
        ]
    )

    def swap(x, bit):
        return lax.ppermute(x, "row", [(r, r ^ bit) for r in range(n_row)])

    last = n_col - 1
    own = [shard[:, :cut], shard[:, cut:]]
    ups, downs = list(own), list(own)
    vals = {}
    pairs = last - 3
    sizes = [1] + [2] * (pairs // 2) + [1] * (pairs % 2) + [1, 1]
    ng = len(sizes)
    ends = [sum(sizes[:n + 1]) for n in range(ng)]
    ties = {}
    for n, end in enumerate(ends[:-1]):
        if n != ng - 3:
            z_at = "R%d" % (end + 4) if end + 4 <= last else "C%d" % (n + 1)
            ties.setdefault(z_at, []).append("Z%d" % n)
        if n < ng - 3:
            w_at = "R%d" % (end + 6) if end + 6 <= last else "C%d" % (ng - 1)
            ties.setdefault(w_at, []).append("W%d" % n)

    def tie(value, target):
        src = [vals[x] for x in ties.get(target, [])]
        return after(value, src) if src else value

    def ring_step(step):
        h = (step - 1) % 2
        up_h, down_h = (0, 1) if step == last else (h, 1 - h)
        ups[up_h], downs[down_h] = tie((ups[up_h], downs[down_h]), "R%d" % step)
        ups[up_h] = lax.ppermute(ups[up_h], "col", up)
        downs[down_h] = lax.ppermute(downs[down_h], "col", down)
        return [ups[up_h], downs[down_h]]

    groups, mine, other = [], [], []
    n0, n1 = ng - 3, ng - 2
    numer_at = {"C%d" % (ng - 1): "N0", "G%d" % (ng - 1): "N1"}

    def through(value, target):
        name = numer_at.get(target)
        if name == "N0":
            vals[name] = numer(flags, (t, fock_vir), groups[:n0], mine[:n0], other[:n0])
        elif name == "N1":
            vals[name] = numer(flags, (vals["N0"],), groups[n0:n1], mine[n0:n1], other[n0:n1])
        if name:
            value, vals[name] = lax.optimization_barrier((value, vals[name]))
        return tie(value, target)

    group, g = list(own), 0
    for step in range(1, last + 1):
        group = group + ring_step(step)
        if step not in ends:
            continue
        group = through(group, "C%d" % g)
        total, send = cross(flags, t, group)
        total = total + swap(send, 1).astype(jnp.float32)
        bit = 2
        while bit < n_row:
            send = total.astype(jnp.bfloat16)
            vals["Z%d" % g] = send
            got = through(swap(send, bit), "G%d" % g)
            total = total + got.astype(jnp.float32)
            bit *= 2
        groups.append(group)
        total = total.astype(jnp.bfloat16)
        vals["W%d" % g] = total
        mine.append(total)
        other.append(swap(total, 1))
        group = []
        g += 1
    acc = vals["N1"]
    return final(flags, eps_occ, acc, t, eps_vir, groups[n1:], mine[n1:], other[n1:])


def solution(mesh):
    placed = (P("row", "col", None, None), P("row", None, "col"), P(), P(), P())
    body = functools.partial(local, mesh.shape["row"], mesh.shape["col"])
    return jax.shard_map(
        body, mesh=mesh, in_specs=placed, out_specs=P("row", "col", None, None), check_vma=False
    )
```

```python
import functools

import jax
import jax.numpy as jnp
from jax import lax
from jax.experimental import pallas as pl
from jax.experimental.pallas import tpu as pltpu
from jax.sharding import PartitionSpec as P

MIB = 1024 * 1024
VMEM = pl.BlockSpec(memory_space=pltpu.VMEM)
SMEM = pl.BlockSpec(memory_space=pltpu.SMEM)


def cost(flops, moved):
    return pl.CostEstimate(
        flops=flops // 1000 + 1, bytes_accessed=moved // 1000 + 1, transcendentals=0
    )


def ring_order(n):
    low = max(d for d in range(1, n + 1) if n % d == 0 and d * d <= n)
    high = n // low
    if low == 1 or high % 2:
        return list(range(n))
    order = [h * low for h in range(high)]
    for turn, h in enumerate(reversed(range(high))):
        lows = range(1, low) if turn % 2 == 0 else range(low - 1, 0, -1)
        order += [h * low + l for l in lows]
    return order


def after(values, gate):
    return lax.optimization_barrier((values, gate))[0]


def cross_kernel(flags, t_ref, *refs):
    chunks, (keep_ref, send_ref) = refs[:-2], refs[-2:]
    occ, vir = t_ref.shape[0], t_ref.shape[2]
    half = vir // 2
    first = flags[0] == 0
    at = 0
    for c in chunks:
        total = None
        for k in range(occ):
            part = jnp.dot(c[k], t_ref[k], preferred_element_type=jnp.float32)
            part = part + jnp.where(flags[2 + k] == 1, c[k].astype(jnp.float32), 0.0)
            total = part if total is None else total + part
        low, high = total[:, :half], total[:, half:]
        rows = slice(at, at + c.shape[1])
        keep_ref[rows, :] = jnp.where(first, low, high)
        send_ref[rows, :] = jnp.where(first, high, low).astype(send_ref.dtype)
        at += c.shape[1]


def cross(flags, t, chunks):
    rows = sum(c.shape[1] for c in chunks)
    occ, _, vir = t.shape
    return pl.pallas_call(
        cross_kernel,
        out_shape=(
            jax.ShapeDtypeStruct((rows, vir // 2), jnp.float32),
            jax.ShapeDtypeStruct((rows, vir // 2), jnp.bfloat16),
        ),
        in_specs=[SMEM] + [VMEM] * (1 + len(chunks)),
        out_specs=(VMEM, VMEM),
        compiler_params=pltpu.CompilerParams(vmem_limit_bytes=20 * MIB),
        cost_estimate=cost(2 * rows * vir * vir * occ, 2 * t.size + 2 * rows * vir * (occ + 2)),
        name="cross",
    )(flags, t, *chunks)


def dressed_rows(flags, mine, other):
    first = flags[0] == 0
    return jnp.concatenate(
        [jnp.where(first, mine, other), jnp.where(first, other, mine)], axis=1
    )


def tiles(vir):
    step = 256 if vir % 256 == 0 else vir
    return [slice(start, start + step) for start in range(0, vir, step)]


def pair_product(chunks, dressed, k, cols):
    left = jnp.concatenate([c[k, :, cols] for c in chunks], axis=0)
    return lax.dot_general(
        left, dressed, (((0,), (0,)), ((), ())), preferred_element_type=jnp.float32
    )


def numer_kernel(n_chunks, n_groups, fresh, flags, *refs):
    refs = list(refs)
    lead = [refs.pop(0) for _ in range(2 if fresh else 1)]
    chunks = [refs.pop(0) for _ in range(n_chunks)]
    mine = [refs.pop(0) for _ in range(n_groups)]
    other = [refs.pop(0) for _ in range(n_groups)]
    out_ref, dressed = refs
    at = 0
    for m, o in zip(mine, other):
        dressed[at:at + m.shape[0], :] = dressed_rows(flags, m[...], o[...])
        at += m.shape[0]
    occ, vir = out_ref.shape[:2]
    for k in range(occ):
        for cols in tiles(vir):
            if fresh:
                total = jnp.dot(
                    lead[0][k, cols, :], lead[1][...], preferred_element_type=jnp.float32
                )
            else:
                total = lead[0][k, cols, :]
            out_ref[k, cols, :] = total + pair_product(chunks, dressed[...], k, cols)


def numer(flags, lead, chunk_groups, mine, other):
    fresh = len(lead) == 2
    chunks = [c for group in chunk_groups for c in group]
    rows = sum(c.shape[1] for c in chunks)
    occ, vir = lead[0].shape[:2]
    operands = [flags, *lead, *chunks, *mine, *other]
    return pl.pallas_call(
        functools.partial(numer_kernel, len(chunks), len(mine), fresh),
        out_shape=jax.ShapeDtypeStruct((occ, vir, vir), jnp.float32),
        in_specs=[SMEM] + [VMEM] * (len(operands) - 1),
        out_specs=VMEM,
        input_output_aliases={} if fresh else {1: 0},
        scratch_shapes=[pltpu.VMEM((rows, vir), jnp.bfloat16)],
        compiler_params=pltpu.CompilerParams(vmem_limit_bytes=30 * MIB),
        cost_estimate=cost(
            2 * occ * vir * vir * (rows + vir * fresh),
            2 * rows * vir * (occ + 1) + 6 * occ * vir * vir,
        ),
        name="numer",
    )(*operands)


def final_kernel(n_chunks, n_groups, flags, eps_occ, acc_ref, t_ref, eps_row, eps_col, *refs):
    refs = list(refs)
    chunks = [refs.pop(0) for _ in range(n_chunks)]
    mine = [refs.pop(0) for _ in range(n_groups)]
    other = [refs.pop(0) for _ in range(n_groups)]
    out_ref, dressed, tile, sems = refs
    at = 0
    for m, o in zip(mine, other):
        dressed[at:at + m.shape[0], :] = dressed_rows(flags, m[...], o[...])
        at += m.shape[0]
    occ, vir = acc_ref.shape[:2]
    second = eps_occ[flags[1]]
    copies = []
    for k in range(occ):
        first = eps_occ[flags[2 + occ] + k]
        for n, cols in enumerate(tiles(vir)):
            total = acc_ref[k, cols, :] + pair_product(chunks, dressed[...], k, cols)
            denom = (eps_col[cols, :] - first) + (eps_row[...] - second)
            new = t_ref[k, cols, :].astype(jnp.float32) - total / denom
            tile[k, cols, :] = new.astype(tile.dtype)
            copy = pltpu.make_async_copy(
                tile.at[k, cols, :], out_ref.at[k, 0, cols, :], sems.at[k, n]
            )
            copy.start()
            copies.append(copy)
    for copy in copies:
        copy.wait()


def final(flags, eps_occ, acc, t, eps_vir, chunk_groups, mine, other):
    occ, vir = acc.shape[:2]
    chunks = [c for group in chunk_groups for c in group]
    rows = sum(c.shape[1] for c in chunks)
    operands = [flags, eps_occ, acc, t, eps_vir[None, :], eps_vir[:, None], *chunks, *mine, *other]
    return pl.pallas_call(
        functools.partial(final_kernel, len(chunks), len(mine)),
        out_shape=jax.ShapeDtypeStruct((occ, 1, vir, vir), t.dtype),
        in_specs=[SMEM, SMEM] + [VMEM] * (len(operands) - 2),
        out_specs=pl.BlockSpec(memory_space=pl.ANY),
        scratch_shapes=[
            pltpu.VMEM((rows, vir), t.dtype),
            pltpu.VMEM((occ, vir, vir), t.dtype),
            pltpu.SemaphoreType.DMA((occ, len(tiles(vir)))),
        ],
        compiler_params=pltpu.CompilerParams(vmem_limit_bytes=24 * MIB),
        cost_estimate=cost(2 * occ * vir * vir * rows, 8 * t.size),
        name="final",
    )(*operands)


def local(n_row, n_col, amplitudes, ints, eps_occ, eps_vir, fock_vir):
    occ = amplitudes.shape[0]
    row, col = lax.axis_index("row"), lax.axis_index("col")
    t = amplitudes[:, 0]
    shard = jnp.swapaxes(ints, 1, 2)
    q = shard.shape[1]
    cut = (q // 2 + 15) // 16 * 16

    order = ring_order(n_col)
    up = [(order[p], order[(p + 1) % n_col]) for p in range(n_col)]
    down = [(b, a) for a, b in up]

    first_ids = row * occ + jnp.arange(occ, dtype=jnp.int32)
    flags = jnp.concatenate(
        [
            jnp.stack([row % 2, col]).astype(jnp.int32),
            (first_ids == col).astype(jnp.int32),
            first_ids[:1],
        ]
    )

    def swap(x, bit):
        return lax.ppermute(x, "row", [(r, r ^ bit) for r in range(n_row)])

    last = n_col - 1
    own = [shard[:, :cut], shard[:, cut:]]
    ups, downs = list(own), list(own)
    vals = {}
    pairs = last - 3
    sizes = [1] + [2] * (pairs // 2) + [1] * (pairs % 2) + [1, 1]
    ng = len(sizes)
    ends = [sum(sizes[:n + 1]) for n in range(ng)]
    ties = {}
    for n, end in enumerate(ends[:-1]):
        if n != ng - 3:
            z_at = "R%d" % (end + 4) if end + 4 < last else "C%d" % min(n + 2, ng - 1)
            ties.setdefault(z_at, []).append("Z%d" % n)
        if n < ng - 3 and end + 6 <= last:
            ties.setdefault("R%d" % (end + 6), []).append("W%d" % n)
    ties.setdefault("R4", []).append("X0")

    def tie(value, target):
        src = [vals[x] for x in ties.get(target, [])]
        return after(value, src) if src else value

    def ring_step(step):
        h = (step - 1) % 2
        up_h, down_h = (0, 1) if step == last else (h, 1 - h)
        ups[up_h], downs[down_h] = tie((ups[up_h], downs[down_h]), "R%d" % step)
        ups[up_h] = lax.ppermute(ups[up_h], "col", up)
        downs[down_h] = lax.ppermute(downs[down_h], "col", down)
        return [ups[up_h], downs[down_h]]

    groups, mine, other = [], [], []
    n0, n1 = ng - 3, ng - 2
    numer_at = {"C%d" % (ng - 1): "N0", "G%d" % (ng - 1): "N1"}

    def through(value, target):
        name = numer_at.get(target)
        if name == "N0":
            vals[name] = numer(flags, (t, fock_vir), groups[:n0], mine[:n0], other[:n0])
        elif name == "N1":
            vals[name] = numer(flags, (vals["N0"],), groups[n0:n1], mine[n0:n1], other[n0:n1])
        if name:
            value, vals[name] = lax.optimization_barrier((value, vals[name]))
        return tie(value, target)

    group, g = list(own), 0
    for step in range(1, last + 1):
        group = group + ring_step(step)
        if step not in ends:
            continue
        group = through(group, "C%d" % g)
        total, send = cross(flags, t, group)
        vals["X%d" % g] = send
        total = total + swap(send, 1).astype(jnp.float32)
        bit = 2
        while bit < n_row:
            send = total.astype(jnp.bfloat16)
            vals["Z%d" % g] = send
            got = through(swap(send, bit), "G%d" % g)
            total = total + got.astype(jnp.float32)
            bit *= 2
        groups.append(group)
        total = total.astype(jnp.bfloat16)
        vals["W%d" % g] = total
        mine.append(total)
        other.append(swap(total, 1))
        group = []
        g += 1
    acc = vals["N1"]
    return final(flags, eps_occ, acc, t, eps_vir, groups[n1:], mine[n1:], other[n1:])


def solution(mesh):
    placed = (P("row", "col", None, None), P("row", None, "col"), P(), P(), P())
    body = functools.partial(local, mesh.shape["row"], mesh.shape["col"])
    return jax.shard_map(
        body, mesh=mesh, in_specs=placed, out_specs=P("row", "col", None, None), check_vma=False
    )
```

```python
import functools

import jax
import jax.numpy as jnp
from jax import lax
from jax.experimental import pallas as pl
from jax.experimental.pallas import tpu as pltpu
from jax.sharding import PartitionSpec as P

MIB = 1024 * 1024
VMEM = pl.BlockSpec(memory_space=pltpu.VMEM)
SMEM = pl.BlockSpec(memory_space=pltpu.SMEM)


def cost(flops, moved):
    return pl.CostEstimate(
        flops=flops // 1000 + 1, bytes_accessed=moved // 1000 + 1, transcendentals=0
    )


def ring_order(n):
    low = max(d for d in range(1, n + 1) if n % d == 0 and d * d <= n)
    high = n // low
    if low == 1 or high % 2:
        return list(range(n))
    order = [h * low for h in range(high)]
    for turn, h in enumerate(reversed(range(high))):
        lows = range(1, low) if turn % 2 == 0 else range(low - 1, 0, -1)
        order += [h * low + l for l in lows]
    return order


def after(values, gate):
    return lax.optimization_barrier((values, gate))[0]


def cross_kernel(flags, t_ref, *refs):
    chunks, (keep_ref, send_ref) = refs[:-2], refs[-2:]
    occ, vir = t_ref.shape[0], t_ref.shape[2]
    half = vir // 2
    first = flags[0] == 0
    at = 0
    for c in chunks:
        total = None
        for k in range(occ):
            part = jnp.dot(c[k], t_ref[k], preferred_element_type=jnp.float32)
            part = part + jnp.where(flags[2 + k] == 1, c[k].astype(jnp.float32), 0.0)
            total = part if total is None else total + part
        low, high = total[:, :half], total[:, half:]
        rows = slice(at, at + c.shape[1])
        keep_ref[rows, :] = jnp.where(first, low, high)
        send_ref[rows, :] = jnp.where(first, high, low).astype(send_ref.dtype)
        at += c.shape[1]


def cross(flags, t, chunks):
    rows = sum(c.shape[1] for c in chunks)
    occ, _, vir = t.shape
    return pl.pallas_call(
        cross_kernel,
        out_shape=(
            jax.ShapeDtypeStruct((rows, vir // 2), jnp.float32),
            jax.ShapeDtypeStruct((rows, vir // 2), jnp.bfloat16),
        ),
        in_specs=[SMEM] + [VMEM] * (1 + len(chunks)),
        out_specs=(VMEM, VMEM),
        compiler_params=pltpu.CompilerParams(vmem_limit_bytes=20 * MIB),
        cost_estimate=cost(2 * rows * vir * vir * occ, 2 * t.size + 2 * rows * vir * (occ + 2)),
        name="cross",
    )(flags, t, *chunks)


def dressed_rows(flags, mine, other):
    first = flags[0] == 0
    return jnp.concatenate(
        [jnp.where(first, mine, other), jnp.where(first, other, mine)], axis=1
    )


def tiles(vir):
    step = 256 if vir % 256 == 0 else vir
    return [slice(start, start + step) for start in range(0, vir, step)]


def pair_product(chunks, dressed, k, cols):
    left = jnp.concatenate([c[k, :, cols] for c in chunks], axis=0)
    return lax.dot_general(
        left, dressed, (((0,), (0,)), ((), ())), preferred_element_type=jnp.float32
    )


def numer_kernel(n_chunks, n_groups, fresh, flags, *refs):
    refs = list(refs)
    lead = [refs.pop(0) for _ in range(2 if fresh else 1)]
    chunks = [refs.pop(0) for _ in range(n_chunks)]
    mine = [refs.pop(0) for _ in range(n_groups)]
    other = [refs.pop(0) for _ in range(n_groups)]
    out_ref, dressed = refs
    at = 0
    for m, o in zip(mine, other):
        dressed[at:at + m.shape[0], :] = dressed_rows(flags, m[...], o[...])
        at += m.shape[0]
    occ, vir = out_ref.shape[:2]
    for k in range(occ):
        for cols in tiles(vir):
            if fresh:
                total = jnp.dot(
                    lead[0][k, cols, :], lead[1][...], preferred_element_type=jnp.float32
                )
            else:
                total = lead[0][k, cols, :]
            out_ref[k, cols, :] = total + pair_product(chunks, dressed[...], k, cols)


def numer(flags, lead, chunk_groups, mine, other):
    fresh = len(lead) == 2
    chunks = [c for group in chunk_groups for c in group]
    rows = sum(c.shape[1] for c in chunks)
    occ, vir = lead[0].shape[:2]
    operands = [flags, *lead, *chunks, *mine, *other]
    return pl.pallas_call(
        functools.partial(numer_kernel, len(chunks), len(mine), fresh),
        out_shape=jax.ShapeDtypeStruct((occ, vir, vir), jnp.float32),
        in_specs=[SMEM] + [VMEM] * (len(operands) - 1),
        out_specs=VMEM,
        input_output_aliases={} if fresh else {1: 0},
        scratch_shapes=[pltpu.VMEM((rows, vir), jnp.bfloat16)],
        compiler_params=pltpu.CompilerParams(vmem_limit_bytes=30 * MIB),
        cost_estimate=cost(
            2 * occ * vir * vir * (rows + vir * fresh),
            2 * rows * vir * (occ + 1) + 6 * occ * vir * vir,
        ),
        name="numer",
    )(*operands)


def final_kernel(n_chunks, n_groups, flags, eps_occ, acc_ref, t_ref, eps_row, eps_col, *refs):
    refs = list(refs)
    chunks = [refs.pop(0) for _ in range(n_chunks)]
    mine = [refs.pop(0) for _ in range(n_groups)]
    other = [refs.pop(0) for _ in range(n_groups)]
    out_ref, dressed, tile, sems = refs
    at = 0
    for m, o in zip(mine, other):
        dressed[at:at + m.shape[0], :] = dressed_rows(flags, m[...], o[...])
        at += m.shape[0]
    occ, vir = acc_ref.shape[:2]
    second = eps_occ[flags[1]]
    copies = []
    for k in range(occ):
        first = eps_occ[flags[2 + occ] + k]
        for n, cols in enumerate(tiles(vir)):
            total = acc_ref[k, cols, :] + pair_product(chunks, dressed[...], k, cols)
            denom = (eps_col[cols, :] - first) + (eps_row[...] - second)
            new = t_ref[k, cols, :].astype(jnp.float32) - total / denom
            tile[k, cols, :] = new.astype(tile.dtype)
            copy = pltpu.make_async_copy(
                tile.at[k, cols, :], out_ref.at[k, 0, cols, :], sems.at[k, n]
            )
            copy.start()
            copies.append(copy)
    for copy in copies:
        copy.wait()


def final(flags, eps_occ, acc, t, eps_vir, chunk_groups, mine, other):
    occ, vir = acc.shape[:2]
    chunks = [c for group in chunk_groups for c in group]
    rows = sum(c.shape[1] for c in chunks)
    operands = [flags, eps_occ, acc, t, eps_vir[None, :], eps_vir[:, None], *chunks, *mine, *other]
    return pl.pallas_call(
        functools.partial(final_kernel, len(chunks), len(mine)),
        out_shape=jax.ShapeDtypeStruct((occ, 1, vir, vir), t.dtype),
        in_specs=[SMEM, SMEM] + [VMEM] * (len(operands) - 2),
        out_specs=pl.BlockSpec(memory_space=pl.ANY),
        scratch_shapes=[
            pltpu.VMEM((rows, vir), t.dtype),
            pltpu.VMEM((occ, vir, vir), t.dtype),
            pltpu.SemaphoreType.DMA((occ, len(tiles(vir)))),
        ],
        compiler_params=pltpu.CompilerParams(vmem_limit_bytes=24 * MIB),
        cost_estimate=cost(2 * occ * vir * vir * rows, 8 * t.size),
        name="final",
    )(*operands)


def local(n_row, n_col, amplitudes, ints, eps_occ, eps_vir, fock_vir):
    occ = amplitudes.shape[0]
    row, col = lax.axis_index("row"), lax.axis_index("col")
    t = amplitudes[:, 0]
    shard = jnp.swapaxes(ints, 1, 2)
    q = shard.shape[1]
    cut = (q // 2 + 15) // 16 * 16

    order = ring_order(n_col)
    up = [(order[p], order[(p + 1) % n_col]) for p in range(n_col)]
    down = [(b, a) for a, b in up]

    first_ids = row * occ + jnp.arange(occ, dtype=jnp.int32)
    flags = jnp.concatenate(
        [
            jnp.stack([row % 2, col]).astype(jnp.int32),
            (first_ids == col).astype(jnp.int32),
            first_ids[:1],
        ]
    )

    def swap(x, bit):
        return lax.ppermute(x, "row", [(r, r ^ bit) for r in range(n_row)])

    last = n_col - 1
    own = [shard[:, :cut], lax.optimization_barrier(shard)[:, cut:]]
    ups, downs = list(own), list(own)
    vals = {}
    pairs = last - 3
    sizes = [1] + [2] * (pairs // 2) + [1] * (pairs % 2) + [1, 1]
    ng = len(sizes)
    ends = [sum(sizes[:n + 1]) for n in range(ng)]
    ties = {}
    for n, end in enumerate(ends[:-1]):
        if n != ng - 3:
            z_at = "R%d" % (end + 4) if end + 4 <= last else "C%d" % (n + 1)
            ties.setdefault(z_at, []).append("Z%d" % n)
        if n < ng - 3:
            w_at = "R%d" % (end + 6) if end + 6 <= last else "C%d" % (ng - 1)
            ties.setdefault(w_at, []).append("W%d" % n)

    def tie(value, target):
        src = [vals[x] for x in ties.get(target, [])]
        return after(value, src) if src else value

    def ring_step(step):
        h = (step - 1) % 2
        up_h, down_h = (0, 1) if step == last else (h, 1 - h)
        ups[up_h], downs[down_h] = tie((ups[up_h], downs[down_h]), "R%d" % step)
        ups[up_h] = lax.ppermute(ups[up_h], "col", up)
        downs[down_h] = lax.ppermute(downs[down_h], "col", down)
        return [ups[up_h], downs[down_h]]

    groups, mine, other = [], [], []
    n0, n1 = ng - 3, ng - 2
    numer_at = {"C%d" % (ng - 1): "N0", "G%d" % (ng - 1): "N1"}

    def through(value, target):
        name = numer_at.get(target)
        if name == "N0":
            vals[name] = numer(flags, (t, fock_vir), groups[:n0], mine[:n0], other[:n0])
        elif name == "N1":
            vals[name] = numer(flags, (vals["N0"],), groups[n0:n1], mine[n0:n1], other[n0:n1])
        if name:
            value, vals[name] = lax.optimization_barrier((value, vals[name]))
        return tie(value, target)

    group, g = list(own), 0
    for step in range(1, last + 1):
        group = group + ring_step(step)
        if step not in ends:
            continue
        group = through(group, "C%d" % g)
        total, send = cross(flags, t, group)
        total = total + swap(send, 1).astype(jnp.float32)
        bit = 2
        while bit < n_row:
            send = total.astype(jnp.bfloat16)
            vals["Z%d" % g] = send
            got = through(swap(send, bit), "G%d" % g)
            total = total + got.astype(jnp.float32)
            bit *= 2
        groups.append(group)
        total = total.astype(jnp.bfloat16)
        vals["W%d" % g] = total
        mine.append(total)
        other.append(swap(total, 1))
        group = []
        g += 1
    acc = vals["N1"]
    return final(flags, eps_occ, acc, t, eps_vir, groups[n1:], mine[n1:], other[n1:])


def solution(mesh):
    placed = (P("row", "col", None, None), P("row", None, "col"), P(), P(), P())
    body = functools.partial(local, mesh.shape["row"], mesh.shape["col"])
    return jax.shard_map(
        body, mesh=mesh, in_specs=placed, out_specs=P("row", "col", None, None), check_vma=False
    )
```
